256 devices in a mesh: lat: 8 (over x, core), lon: 8 (over z), dep: 4 (over y).
Axes of the slice: x: 4, y: 4, z: 8, core: 2. Of those that a mesh axis runs over, the one named last changes fastest.
Arguments:
- kernels: bfloat16 [524288, 6, 128], P(('lat', 'lon', 'dep')), may hold values from -6 to 6
- basis_weights: bfloat16 [8, 128, 128], replicated, may hold values from -0.5 to 0.5
- owner_block: int32 [524288, 1], P(('lat', 'lon', 'dep')), may hold values from 0 to 63; in each aligned block of 2048 rows (0 to 2047, 2048 to 4095, ...) at most 64 rows name the same one
- column_offset: int32 [524288], P(('lat', 'lon', 'dep')), may hold values from 0 to 63
- basis_index: int32 [524288], P(('lat', 'lon', 'dep')), may hold values from 0 to 7
Outputs:
- projected: float32 [6, 64, 64, 512], P(None, 'lat', 'lon', 'dep')
- smoothed: float32 [6, 64, 64, 512], P(None, 'lat', 'lon', 'dep')
The draws below stay inside these ranges and needn't reach their ends.
Inputs may be any that keep to these rules, and one draw needn't show every extreme that they name: `owner_block`: among the rows of one device, no block is named more than 64 times, and some block is named exactly 64 times.
All inputs are finite; a program needn't handle non-finite values.
Results may differ from the reference program's by a relative error of at most 0.0003.
Values sent between devices are 32-bit elements; how exact they have to be, the bound alone decides.
No kernel may reach another device: no remote copies, remote signals or barrier semaphores. Data moves between devices by JAX's collectives and lax.ppermute only.
A program may use at most 128 MiB of HBM per device.

```python
import math
import jax
import jax.numpy as jnp
import numpy as np
from jax import lax

E_DEV = 2048
KERN = 6
NPT = 128
NB = 8
GX = 8
GY = 8
GZ = 128
RADIUS = 4
NTILE = 64
CAP = 64
ELEMS = 524288
NX = 64
NY = 64
NZ = 512
N_LAT = 8
N_LON = 8
N_DEP = 4
DEVICES = 256


def touch_ends(entries, rng, low, high):
    extent = entries.shape
    spot = [jax.random.randint(jax.random.fold_in(rng, axis), (), 0, extent[axis]) for axis in range(len(extent))]
    entries = entries.at[tuple(spot)].set(low)
    longest = extent.index(max(extent))
    spot[longest] = (spot[longest] + 1) % extent[longest]
    return entries.at[tuple(spot)].set(high)


def levels(rng, shape, shards, low, high):
    def one(dim, shards_of):
        draws = jax.random.uniform(jax.random.fold_in(jax.random.fold_in(rng, 6), dim), (shards_of,), jnp.float32, low / len(shards), high / len(shards))
        return jnp.repeat(jnp.exp(draws), shape[dim] // shards_of).reshape((-1,) + (1,) * (len(shape) - dim - 1))

    gain = one(*shards[0])
    for cut in shards[1:]:
        gain = gain * one(*cut)
    return gain


def routed_block(key, own, number, rows, amount, top, bound, slope):
    ranking = jax.random.permutation(key, amount)
    packed, usual = shares(amount, rows * top, bound, slope, True), shares(amount, rows * top, bound, slope, False)
    places = jnp.arange(amount)

    def named(tallies, offset_by):
        used = int((tallies > 0).sum())
        fixed = max(1, used // 4)
        shifted = fixed + (places - fixed + offset_by * (used - fixed)) % max(1, amount - fixed)
        return jnp.zeros((amount,), jnp.int32).at[ranking[jnp.where(places < fixed, places, shifted)]].set(jnp.asarray(tallies, jnp.int32))

    tallies = jnp.where(number % 4 == 0, named(packed, number // 4), named(usual, number - number // 4 - 1))
    mixed = jax.random.permutation(jax.random.fold_in(own, 3), amount)
    donor, taker = mixed[0:amount // 2 * 2:2], mixed[1:amount // 2 * 2:2]
    margin = jnp.minimum(tallies[donor] - 1, bound - tallies[taker]) // 2
    margin = jnp.where((donor == ranking[0]) | (taker == ranking[0]) | (tallies[taker] == 0), 0, jnp.maximum(margin, 0))
    shifted = jax.random.randint(jax.random.fold_in(own, 4), (amount // 2,), 0, 1 << 20) % (margin + 1)
    tallies = tallies.at[donor].add(-shifted).at[taker].add(shifted)
    members = jnp.searchsorted(jnp.cumsum(tallies), jnp.arange(rows * top), side="right").astype(jnp.int32)
    table = members.reshape(top, rows).T
    table = table[jax.random.permutation(jax.random.fold_in(own, 1), rows)]
    offset_by = jax.random.randint(jax.random.fold_in(own, 2), (rows, 1), 0, top)
    return jnp.take_along_axis(table, (jnp.arange(top)[None, :] + offset_by) % top, axis=1)


def shares(amount, total, limit, skew, full):
    portions = [(1 << 20) // math.isqrt(grade ** skew) + 1 for grade in range(1, amount + 1)]
    largest = limit if full else min(limit, max(-(-total // amount), total * portions[0] // sum(portions)))
    least = 1 if total - largest >= amount - 1 else 0
    counts, spare = [largest] + [least] * (amount - 1), total - largest - least * (amount - 1)
    while spare > 0:
        candidates = [i for i in range(1, amount) if counts[i] < largest] or [i for i in range(1, amount) if counts[i] < limit]
        mass, left = sum([portions[i] for i in candidates]), spare
        for i in candidates:
            more = min(limit - counts[i], max(1, left * portions[i] // mass), spare)
            counts[i] = counts[i] + more
            spare = spare - more
    return np.array(counts)


def bell_draw(stream_key, dims, width, bound, shards=(), kind=jnp.bfloat16):
    values = width * jax.random.normal(stream_key, dims, jnp.float32)
    if shards:
        values = values * levels(stream_key, dims, shards, -0.22, 0.18)
    return jnp.clip(values, -bound, bound).astype(kind)


def setup_inputs(seed: int = 0) -> dict:
    arg_keys = jax.random.split(jax.random.key(seed), 6)
    kernels = bell_draw(arg_keys[0], (ELEMS, KERN, NPT), 1.0, 6.0, ((0, 256),))
    basis_weights = bell_draw(arg_keys[1], (NB, NPT, GZ), NPT ** -0.5, 0.5)
    owner_block_keys = jax.random.split(jax.random.fold_in(arg_keys[2], 1), ELEMS // E_DEV)
    owner_block_turns = jax.random.permutation(jax.random.fold_in(arg_keys[2], 3), ELEMS // E_DEV)
    owner_block = jax.vmap(lambda own, number: routed_block(jax.random.fold_in(arg_keys[2], 2), own, number, E_DEV, N_LAT * N_LON, 1, CAP, 2))(owner_block_keys, owner_block_turns).reshape((ELEMS, 1))
    column_offset = touch_ends(jax.random.randint(arg_keys[3], (ELEMS,), 0, NTILE), jax.random.fold_in(arg_keys[3], 1), 0, NTILE - 1).astype(jnp.int32)
    basis_index = touch_ends(jax.random.randint(arg_keys[4], (ELEMS,), 0, NB), jax.random.fold_in(arg_keys[4], 1), 0, NB - 1).astype(jnp.int32)
    return dict(kernels=kernels, basis_weights=basis_weights, owner_block=owner_block, column_offset=column_offset, basis_index=basis_index)


def gauss_taps():
    weights = [math.exp(-(offset * offset) / 8.0) for offset in range(-RADIUS, RADIUS + 1)]
    total = 0.0
    for value in weights:
        total = total + value
    return [value / total for value in weights]


def smooth_along(field, axis_pos):
    widths = [(0, 0)] * field.ndim
    widths[axis_pos] = (RADIUS, RADIUS)
    padded = jnp.pad(field, widths)
    length = field.shape[axis_pos]
    result = jnp.zeros_like(field)
    for place, factor in enumerate(gauss_taps()):
        result = result + factor * lax.slice_in_dim(padded, place, place + length, axis=axis_pos)
    return result


def reference(kernels, basis_weights, owner_block, column_offset, basis_index):
    model_grid = jnp.zeros((KERN, NX, NY, N_DEP, GZ), jnp.float32)

    def per_device(grid_now, device):
        start = (device * E_DEV).astype(jnp.int32)
        kernel_rows = lax.dynamic_slice_in_dim(kernels, start, E_DEV, 0).astype(jnp.float32)
        owners = lax.dynamic_slice_in_dim(owner_block, start, E_DEV, 0)[:, 0]
        offsets = lax.dynamic_slice_in_dim(column_offset, start, E_DEV, 0)
        chosen = lax.dynamic_slice_in_dim(basis_index, start, E_DEV, 0)
        weights = basis_weights[chosen].astype(jnp.float32)
        contribution = jnp.einsum("ecp,epz->ecz", kernel_rows, weights, precision=lax.Precision.HIGHEST)
        xcells = (owners // N_LON) * GX + offsets // GY
        ycells = (owners % N_LON) * GY + offsets % GY
        layers = jnp.zeros_like(owners) + (device % N_DEP).astype(jnp.int32)
        grid_now = grid_now.at[:, xcells, ycells, layers, :].add(jnp.transpose(contribution, (1, 0, 2)))
        return grid_now, None

    model_grid, _ = lax.scan(per_device, model_grid, jnp.arange(DEVICES, dtype=jnp.int32))
    projected = model_grid.reshape(KERN, NX, NY, NZ)
    along_lat = smooth_along(projected, 1)
    along_lon = smooth_along(along_lat, 2)
    smoothed = smooth_along(along_lon, 3)
    return projected, smoothed
```

```python
import functools
import math

import jax
import jax.numpy as jnp
import numpy as np
from jax import lax
from jax.experimental import pallas as pl
from jax.experimental.pallas import tpu as pltpu
from jax.sharding import PartitionSpec as P

GX = 8
GY = 8
RADIUS = 4
CHIPS = 4
LON = 8
CHUNK = 64
WIDTH = 32
UNROLL = 16

CORE = [(i, i ^ 1) for i in range(2 * CHIPS)]
RING_X = [(2 * x + c, 2 * ((x + 1 - 2 * c) % CHIPS) + c) for x in range(CHIPS) for c in range(2)]
RING_Z = [
    (lat * LON + z, lat * LON + (z + 1 - 2 * (lat % 2)) % LON)
    for lat in range(2 * CHIPS)
    for z in range(LON)
]

MINE_A = [(3, 0), (2, 0), (1, 0), (0, 1), (1, 1), (2, 1), (3, 1), (4, 1)]
THEIRS_A = [(5, 1), (6, 1), (7, 1), (0, 0), (7, 0), (6, 0), (5, 0), (4, 0)]
LAYOUT_A = (
    [(2, q, 1) for q in range(LON)]
    + [(1, q, own) for q, own in MINE_A + THEIRS_A]
    + [(0, q, own) for q, own in MINE_A]
)
MINE_B = [(1, 0), (0, 1), (1, 1), (2, 1)]
THEIRS_B = [(3, 1), (0, 0), (3, 0), (2, 0)]
LAYOUT_B = (
    [(p, 4, 1) for p in range(CHIPS)]
    + [(p, q, own) for q in (3, 2, 1) for p, own in MINE_B + THEIRS_B]
    + [(p, 0, own) for p, own in MINE_B]
)
PARTS_A = (8, 16, 8)
PARTS_B = (4, 8, 8, 8, 4)


def block_tables():
    table = np.zeros((2 * CHIPS, LON, 2, 2 * CHIPS * LON), np.int32)
    for lat in range(2 * CHIPS):
        for z in range(LON):
            for owner in range(2 * CHIPS * LON):
                core = owner // LON % 2
                dx = (owner // LON // 2 - lat // 2) % CHIPS
                dz = (owner % LON - z) % LON
                by_x = {0: None, 1: 0, 2: core, 3: 1}[dx]
                by_z = {0: None, 4: core}.get(dz, 0 if dz < 4 else 1)
                for half, (first, second, layout) in enumerate(
                    ((by_x, by_z, LAYOUT_A), (by_z, by_x, LAYOUT_B))
                ):
                    handler = first if first is not None else second if second is not None else core
                    sign = 1 - 2 * handler
                    place = layout.index((dx * sign % CHIPS, dz * sign % LON, int(core == handler)))
                    table[lat, z, half, owner] = (
                        half * 64 + (0 if handler == lat % 2 else 32) + place
                    )
    return table * (6 * WIDTH)


def project_kernel(
    sizes, kernels_ref, weights_ref, owner_ref, column_ref, basis_ref, table_ref, *rest
):
    outs = rest[: len(sizes)]
    pos_v, row_v, end_v, pos_s, row_s, end_s, stage, acc, sems, copy_sems = rest[len(sizes) :]
    rows, lanes = owner_ref.shape
    elems = rows * lanes
    basis_count = weights_ref.shape[0]
    channels = kernels_ref.shape[1]

    owner = owner_ref[...]
    column = column_ref[...]
    first = jnp.zeros((rows, lanes), jnp.int32)
    second = jnp.zeros((rows, lanes), jnp.int32)
    for o in range(table_ref.shape[1]):
        hit = owner == o
        first = jnp.where(hit, table_ref[0, o], first)
        second = jnp.where(hit, table_ref[1, o], second)
    row_v[...] = jnp.where(column < WIDTH, first + column, second + column - WIDTH)

    basis = basis_ref[...]
    upper = (
        lax.broadcasted_iota(jnp.int32, (lanes, lanes), 0)
        <= lax.broadcasted_iota(jnp.int32, (lanes, lanes), 1)
    ).astype(jnp.float32)
    lower = (
        lax.broadcasted_iota(jnp.int32, (rows, rows), 1)
        < lax.broadcasted_iota(jnp.int32, (rows, rows), 0)
    ).astype(jnp.float32)
    base = jnp.zeros((1, lanes), jnp.int32)
    pos = jnp.zeros((rows, lanes), jnp.int32)
    for b in range(basis_count):
        hit = basis == b
        inside = jnp.dot(hit.astype(jnp.float32), upper, preferred_element_type=jnp.float32)
        in_row = jnp.broadcast_to(inside[:, lanes - 1 :], (rows, lanes))
        before = jnp.dot(lower, in_row, preferred_element_type=jnp.float32)
        rank = (before + inside).astype(jnp.int32) - 1
        total = (before + in_row)[rows - 1 :].astype(jnp.int32)
        pos = jnp.where(hit, base + rank, pos)
        base = base + (total + CHUNK - 1) // CHUNK * CHUNK
        end_v[pl.ds(b, 1), :] = base // CHUNK
    pos_v[...] = pos
    loads = [
        pltpu.make_async_copy(pos_v, pos_s, sems.at[0]),
        pltpu.make_async_copy(row_v, row_s, sems.at[1]),
        pltpu.make_async_copy(end_v, end_s, sems.at[2]),
    ]
    for load in loads:
        load.start()

    def clear(i, _):
        acc[pl.ds(pl.multiple_of(i * 512, 512), 512), :] = jnp.zeros((512, 128), jnp.float32)
        return 0

    lax.fori_loop(0, acc.shape[0] // 512, clear, 0)
    for load in loads:
        load.wait()

    per_row = lanes // UNROLL

    def order(i, _):
        r = i // per_row
        c = i % per_row * UNROLL
        for j in range(UNROLL):
            stage[pos_s[r, c + j], pl.ds(0, channels), :] = kernels_ref[i * UNROLL + j].astype(
                jnp.float32
            )
        return 0

    lax.fori_loop(0, elems // UNROLL, order, 0)

    def multiply(b):
        weight = weights_ref[b].astype(jnp.float32)

        def one(k, _):
            part = stage[pl.ds(k * CHUNK, CHUNK)].reshape(CHUNK * 8, lanes)
            stage[pl.ds(k * CHUNK, CHUNK)] = jnp.dot(
                part, weight, preferred_element_type=jnp.float32
            ).reshape(CHUNK, 8, lanes)
            return 0

        lax.fori_loop(0 if b == 0 else end_s[b - 1, 0], end_s[b, 0], one, 0)

    for b in range(basis_count):
        multiply(b)

    def scatter(i, _):
        r = i // per_row
        c = i % per_row * UNROLL
        for j in range(UNROLL):
            where = pl.ds(row_s[r, c + j], channels, stride=WIDTH)
            acc[where, :] += stage[pos_s[r, c + j], pl.ds(0, channels), :]
        return 0

    lax.fori_loop(0, elems // UNROLL, scatter, 0)

    copies = []
    start = 0
    for k, (out, size) in enumerate(zip(outs, sizes)):
        copies.append(
            pltpu.make_async_copy(acc.at[pl.ds(start, size)], out, copy_sems.at[k])
        )
        start += size
    for copy in copies:
        copy.start()
    for copy in copies:
        copy.wait()


def project(kernels, basis_weights, owner, column, basis, table):
    elems, channels, points = kernels.shape
    counts = PARTS_A + PARTS_A + PARTS_B + PARTS_B
    sizes = [count * channels * WIDTH for count in counts]
    rows = elems // 128
    vmem = pl.BlockSpec(memory_space=pltpu.VMEM)
    outs = pl.pallas_call(
        functools.partial(project_kernel, sizes),
        out_shape=[jax.ShapeDtypeStruct((size, 128), jnp.float32) for size in sizes],
        in_specs=[vmem] * 5 + [pl.BlockSpec(memory_space=pltpu.SMEM)],
        out_specs=[pl.BlockSpec(memory_space=pl.ANY)] * len(sizes),
        scratch_shapes=[
            pltpu.VMEM((rows, 128), jnp.int32),
            pltpu.VMEM((rows, 128), jnp.int32),
            pltpu.VMEM((8, 128), jnp.int32),
            pltpu.SMEM((rows, 128), jnp.int32),
            pltpu.SMEM((rows, 128), jnp.int32),
            pltpu.SMEM((8, 128), jnp.int32),
            pltpu.VMEM((elems + 8 * CHUNK, 8, 128), jnp.float32),
            pltpu.VMEM((128 * 6 * WIDTH, 128), jnp.float32),
            pltpu.SemaphoreType.DMA((3,)),
            pltpu.SemaphoreType.DMA((len(sizes),)),
        ],
        compiler_params=pltpu.CompilerParams(vmem_limit_bytes=48 * 1024 * 1024),
        name="project",
    )(
        kernels,
        basis_weights,
        owner.reshape(rows, 128),
        column.reshape(rows, 128),
        basis.reshape(rows, 128),
        table,
    )
    return [
        out.reshape(count, channels, WIDTH, 128) for out, count in zip(outs, counts)
    ]


def over_core(value):
    return lax.ppermute(value, "lat", CORE)


def over_x(value):
    return lax.ppermute(value, "lat", RING_X)


def over_z(value):
    return lax.ppermute(value, ("lat", "lon"), RING_Z)


def gauss_taps():
    weights = [math.exp(-(offset * offset) / 8.0) for offset in range(-RADIUS, RADIUS + 1)]
    total = 0.0
    for value in weights:
        total = total + value
    return [value / total for value in weights]


def pass_along(padded, axis_pos):
    length = padded.shape[axis_pos] - 2 * RADIUS
    result = None
    for place, factor in enumerate(gauss_taps()):
        term = factor * lax.slice_in_dim(padded, place, place + length, axis=axis_pos)
        result = term if result is None else result + term
    return result


def with_halo(block, axis, dim, width):
    count = lax.axis_size(axis)
    forward = [(i, i + 1) for i in range(count - 1)]
    backward = [(target, source) for source, target in forward]
    low = lax.ppermute(
        lax.slice_in_dim(block, block.shape[dim] - width, None, axis=dim), axis, forward
    )
    high = lax.ppermute(lax.slice_in_dim(block, 0, width, axis=dim), axis, backward)
    return jnp.concatenate([low, block, high], axis=dim)


def local(kernels, basis_weights, owner_block, column_offset, basis_index):
    lat = lax.axis_index("lat")
    lon = lax.axis_index("lon")
    table = lax.dynamic_slice(
        jnp.asarray(block_tables()), (lat, lon, 0, 0), (1, 1, 2, 64)
    ).reshape(2, 64)
    parts = project(
        kernels, basis_weights, owner_block, column_offset, basis_index, table
    )
    keep_a, send_a = parts[0:3], parts[3:6]
    keep_b, send_b = parts[6:11], parts[11:16]

    p2, q4 = keep_a[0] + over_core(send_a[0]), keep_b[0] + over_core(send_b[0])
    x_in, z_in = over_x(p2), over_z(q4)
    p1, q3 = keep_a[1] + over_core(send_a[1]), keep_b[1] + over_core(send_b[1])
    q2 = keep_b[2] + over_core(send_b[2])
    q1 = keep_b[3] + over_core(send_b[3])
    p0 = keep_a[2] + over_core(send_a[2])
    q0 = keep_b[4] + over_core(send_b[4])
    p1 = jnp.concatenate([p1[:3], p1[3:11] + x_in, p1[11:]])
    q3 = jnp.concatenate([q3[:1], q3[1:5] + z_in, q3[5:]])
    x_in = over_x(p1)
    q2 = q2 + over_z(q3)
    q1 = q1 + over_z(q2)
    z_in = over_z(q1)
    a = p0 + x_in[:8] + over_core(x_in[8:])
    b = q0 + z_in[:4] + over_core(z_in[4:])

    v = jnp.stack([a[6] + over_z(a[7]), a[0]])
    v = jnp.stack([a[5], a[1]]) + over_z(v)
    v = jnp.stack([a[4], a[2]]) + over_z(v)
    v = over_z(v)
    final_a = a[3] + v[0] + over_core(v[1])
    w = jnp.stack([b[2] + over_x(b[3]), b[0]])
    w = over_x(w)
    final_b = b[1] + w[0] + over_core(w[1])

    channels = kernels.shape[1]
    final_a = final_a.reshape(channels, GX // 2, GY, 128)
    final_b = final_b.reshape(channels, GX // 2, GY, 128)
    projected = jnp.concatenate([final_a, final_b], axis=1)

    even = lat % 2 == 0
    outward = [
        (2 * x + c, 2 * (x + 2 * c - 1) + 1 - c)
        for x in range(CHIPS)
        for c in range(2)
        if 0 <= x + 2 * c - 1 < CHIPS
    ]
    outer = lax.ppermute(jnp.where(even, final_a, final_b), "lat", outward)
    inner = over_core(jnp.where(even, final_b, final_a))
    along_lat = pass_along(
        jnp.concatenate(
            [jnp.where(even, outer, inner), projected, jnp.where(even, inner, outer)], axis=1
        ),
        1,
    )
    along_lon = pass_along(with_halo(along_lat, "lon", 2, RADIUS), 2)
    smoothed = pass_along(with_halo(along_lon, "dep", 3, RADIUS), 3)
    return (projected, smoothed)


def solution(mesh):
    placed = (
        P(("lat", "lon", "dep"), None, None),
        P(),
        P(("lat", "lon", "dep"), None),
        P(("lat", "lon", "dep")),
        P(("lat", "lon", "dep")),
    )
    return jax.shard_map(
        local,
        mesh=mesh,
        in_specs=placed,
        out_specs=(P(None, "lat", "lon", "dep"), P(None, "lat", "lon", "dep")),
        check_vma=False,
    )
```

```python
import math

import jax
import jax.numpy as jnp
import numpy as np
from jax import lax
from jax.experimental import pallas as pl
from jax.experimental.pallas import tpu as pltpu
from jax.sharding import PartitionSpec as P

GX = 8
GY = 8
RADIUS = 4
CHIPS = 4
LON = 8
CHUNK = 128
COLS = (5, 3)
GROUP = 4

CORE = [(i, i ^ 1) for i in range(2 * CHIPS)]
RING_X = [(2 * x + c, 2 * ((x + 1 - 2 * c) % CHIPS) + c) for x in range(CHIPS) for c in range(2)]
RING_Z = [
    (lat * LON + z, lat * LON + (z + 1 - 2 * (lat % 2)) % LON)
    for lat in range(2 * CHIPS)
    for z in range(LON)
]

A_P2 = [[(3, 1), (4, 1), (5, 1)], [(0, 1), (1, 1), (2, 1), (6, 1), (7, 1)]]
A_MINE = [[(3, 0), (3, 1), (4, 1)], [(2, 0), (1, 0), (0, 1), (1, 1), (2, 1)]]
A_THEIRS = [[(5, 1), (5, 0), (4, 0)], [(6, 1), (7, 1), (0, 0), (7, 0), (6, 0)]]
LAYOUT_A = (
    [(2, q, own) for part in A_P2 for q, own in part]
    + [(1, q, own) for mine, theirs in zip(A_MINE, A_THEIRS) for q, own in mine + theirs]
    + [(0, q, own) for mine in A_MINE for q, own in mine]
)
B_MINE = [(1, 0), (0, 1), (1, 1), (2, 1)]
B_THEIRS = [(3, 1), (0, 0), (3, 0), (2, 0)]
LAYOUT_B = (
    [(p, 4, 1) for p in range(CHIPS)]
    + [(p, q, own) for q in (3, 2, 1) for p, own in B_MINE + B_THEIRS]
    + [(p, 0, own) for p, own in B_MINE]
)
PARTS_A = (3, 5, 6, 10, 3, 5)
PARTS_B = (4, 8, 8, 8, 4)


def block_tables():
    table = np.zeros((2 * CHIPS, LON, 2, 2 * CHIPS * LON), np.int32)
    for lat in range(2 * CHIPS):
        for z in range(LON):
            for owner in range(2 * CHIPS * LON):
                core = owner // LON % 2
                dx = (owner // LON // 2 - lat // 2) % CHIPS
                dz = (owner % LON - z) % LON
                by_x = {0: None, 1: 0, 2: core, 3: 1}[dx]
                by_z = {0: None, 4: core}.get(dz, 0 if dz < 4 else 1)
                for half, (first, second, layout) in enumerate(
                    ((by_x, by_z, LAYOUT_A), (by_z, by_x, LAYOUT_B))
                ):
                    handler = first if first is not None else second if second is not None else core
                    sign = 1 - 2 * handler
                    place = layout.index((dx * sign % CHIPS, dz * sign % LON, int(core == handler)))
                    block = (0 if handler == lat % 2 else 32) + place
                    table[lat, z, half, owner] = GY * (
                        64 * COLS[0] * half + block * COLS[half]
                    )
    return table


def project_kernel(
    kernels_ref,
    weights_ref,
    owner_ref,
    column_ref,
    basis_ref,
    table_ref,
    acc,
    raw,
    plain,
    stage,
    pos_v,
    row_v,
    end_v,
    pos_s,
    row_s,
    end_s,
    raw_sems,
    sems,
):
    rows, lanes = owner_ref.shape
    basis_count = weights_ref.shape[0]
    channels, elems, _ = kernels_ref.shape
    pitch = plain.shape[0] // channels

    fetches = [
        pltpu.make_async_copy(kernels_ref.at[c], raw.at[c], raw_sems.at[c])
        for c in range(channels)
    ]
    for fetch in fetches:
        fetch.start()

    owner = owner_ref[...]
    column = column_ref[...]
    first = jnp.zeros((rows, lanes), jnp.int32)
    second = jnp.zeros((rows, lanes), jnp.int32)
    for o in range(table_ref.shape[1]):
        hit = owner == o
        first = jnp.where(hit, table_ref[0, o], first)
        second = jnp.where(hit, table_ref[1, o], second)
    width = GY * COLS[0]
    row = jnp.where(column < width, first + column, second + column - width)
    row_v[...] = row * channels

    basis = basis_ref[...]
    upper = (
        lax.broadcasted_iota(jnp.int32, (lanes, lanes), 0)
        <= lax.broadcasted_iota(jnp.int32, (lanes, lanes), 1)
    ).astype(jnp.float32)
    lower = (
        lax.broadcasted_iota(jnp.int32, (rows, rows), 1)
        < lax.broadcasted_iota(jnp.int32, (rows, rows), 0)
    ).astype(jnp.float32)
    base = jnp.zeros((1, lanes), jnp.int32)
    pos = jnp.zeros((rows, lanes), jnp.int32)
    for b in range(basis_count):
        hit = basis == b
        inside = jnp.dot(hit.astype(jnp.float32), upper, preferred_element_type=jnp.float32)
        in_row = jnp.broadcast_to(inside[:, lanes - 1 :], (rows, lanes))
        before = jnp.dot(lower, in_row, preferred_element_type=jnp.float32)
        rank = (before + inside).astype(jnp.int32) - 1
        total = (before + in_row)[rows - 1 :].astype(jnp.int32)
        pos = jnp.where(hit, base + rank, pos)
        base = base + (total + CHUNK - 1) // CHUNK * CHUNK
        end_v[pl.ds(b, 1), :] = base // CHUNK
    pos_v[...] = pos * channels
    loads = [
        pltpu.make_async_copy(source, target, sems.at[i])
        for i, (source, target) in enumerate(
            ((pos_v, pos_s), (row_v, row_s), (end_v, end_s))
        )
    ]
    for load in loads:
        load.start()

    def clear(i, _):
        acc[pl.ds(pl.multiple_of(i * 512, 512), 512), :] = jnp.zeros((512, 128), jnp.float32)
        return 0

    lax.fori_loop(0, acc.shape[0] // 512, clear, 0)

    for c, fetch in enumerate(fetches):
        fetch.wait()

        def widen(i, _):
            start = pl.multiple_of(i * 256, 256)
            plain[pl.ds(c * pitch + start, 256), :] = raw[c, pl.ds(start, 256), :].astype(
                jnp.float32
            )
            return 0

        lax.fori_loop(0, elems // 256, widen, 0)
    for load in loads:
        load.wait()

    def order(r, _):
        for j in range(lanes):
            stage[pl.ds(pos_s[r, j], channels), :] = plain[
                pl.ds(r * lanes + j, channels, stride=pitch), :
            ]
        return 0

    lax.fori_loop(0, rows, order, 0)

    def multiply(b):
        weight = weights_ref[b]

        def one(k, _):
            where = pl.ds(pl.multiple_of(k * (CHUNK * channels), CHUNK * channels), CHUNK * channels)
            stage[where, :] = jnp.dot(
                stage[where, :].astype(jnp.bfloat16), weight, preferred_element_type=jnp.float32
            )
            return 0

        lax.fori_loop(0 if b == 0 else end_s[b - 1, 0], end_s[b, 0], one, 0)

    for b in range(basis_count):
        multiply(b)

    def scatter(r, _):
        for j in range(0, lanes, GROUP):
            targets = [row_s[r, j + i] for i in range(GROUP)]
            sums = [acc[pl.ds(target, channels), :] for target in targets]
            terms = [stage[pl.ds(pos_s[r, j + i], channels), :] for i in range(GROUP)]
            for i in range(GROUP):
                sums[i] = sums[i] + terms[i]
                for h in range(i):
                    sums[i] = sums[i] + jnp.where(targets[i] == targets[h], terms[h], 0.0)
            for target, value in zip(targets, sums):
                acc[pl.ds(target, channels), :] = value
        return 0

    lax.fori_loop(0, rows, scatter, 0)


def project(kernels, basis_weights, owner, column, basis, table):
    elems, channels, points = kernels.shape
    rows = elems // 128
    room = elems + 8 * CHUNK
    pitch = elems + 8
    vmem = pl.BlockSpec(memory_space=pltpu.VMEM)
    total = 64 * GX * GY * channels
    acc = pl.pallas_call(
        project_kernel,
        out_shape=pltpu.VMEM((total, 128), jnp.float32),
        in_specs=[pl.BlockSpec(memory_space=pl.ANY)]
        + [vmem] * 4
        + [pl.BlockSpec(memory_space=pltpu.SMEM)],
        out_specs=vmem,
        scratch_shapes=[
            pltpu.VMEM((channels, elems, 128), jnp.bfloat16),
            pltpu.VMEM((channels * pitch, 128), jnp.float32),
            pltpu.VMEM((channels * room, 128), jnp.float32),
            pltpu.VMEM((rows, 128), jnp.int32),
            pltpu.VMEM((rows, 128), jnp.int32),
            pltpu.VMEM((8, 128), jnp.int32),
            pltpu.SMEM((rows, 128), jnp.int32),
            pltpu.SMEM((rows, 128), jnp.int32),
            pltpu.SMEM((8, 128), jnp.int32),
            pltpu.SemaphoreType.DMA((channels,)),
            pltpu.SemaphoreType.DMA((3,)),
        ],
        compiler_params=pltpu.CompilerParams(vmem_limit_bytes=48 * 1024 * 1024),
        name="project",
    )(
        jnp.transpose(kernels, (1, 0, 2)),
        basis_weights,
        owner.reshape(rows, 128),
        column.reshape(rows, 128),
        basis.reshape(rows, 128),
        table,
    )
    parts = []
    start = 0
    for counts, cols in ((PARTS_A * 2, COLS[0]), (PARTS_B * 2, COLS[1])):
        size = cols * GY * channels
        for count in counts:
            parts.append(acc[start : start + count * size].reshape(count, size, 128))
            start += count * size
    return parts


def over_core(value):
    return lax.ppermute(value, "lat", CORE)


def over_x(value):
    return lax.ppermute(value, "lat", RING_X)


def over_z(value):
    return lax.ppermute(value, ("lat", "lon"), RING_Z)


def add_at(block, part, start):
    end = start + part.shape[0]
    return jnp.concatenate([block[:start], block[start:end] + part, block[end:]])


def gauss_taps():
    weights = [math.exp(-(offset * offset) / 8.0) for offset in range(-RADIUS, RADIUS + 1)]
    total = 0.0
    for value in weights:
        total = total + value
    return [value / total for value in weights]


def pass_along(padded, axis_pos):
    length = padded.shape[axis_pos] - 2 * RADIUS
    result = None
    for place, factor in enumerate(gauss_taps()):
        term = factor * lax.slice_in_dim(padded, place, place + length, axis=axis_pos)
        result = term if result is None else result + term
    return result


def with_halo(block, axis, dim, width):
    count = lax.axis_size(axis)
    forward = [(i, i + 1) for i in range(count - 1)]
    backward = [(target, source) for source, target in forward]
    low = lax.ppermute(
        lax.slice_in_dim(block, block.shape[dim] - width, None, axis=dim), axis, forward
    )
    high = lax.ppermute(lax.slice_in_dim(block, 0, width, axis=dim), axis, backward)
    return jnp.concatenate([low, block, high], axis=dim)


def local(kernels, basis_weights, owner_block, column_offset, basis_index):
    lat = lax.axis_index("lat")
    lon = lax.axis_index("lon")
    table = lax.dynamic_slice(
        jnp.asarray(block_tables()), (lat, lon, 0, 0), (1, 1, 2, 64)
    ).reshape(2, 64)
    parts = project(
        kernels, basis_weights, owner_block, column_offset, basis_index, table
    )
    keep_a, send_a = parts[0:6], parts[6:12]
    keep_b, send_b = parts[12:17], parts[17:22]

    p2 = [keep_a[0] + over_core(send_a[0]), None]
    q4 = keep_b[0] + over_core(send_b[0])
    z_in = over_z(q4)
    x_in = [over_x(p2[0]), None]
    p2[1] = keep_a[1] + over_core(send_a[1])
    x_in[1] = over_x(p2[1])
    p1 = [keep_a[2 + i] + over_core(send_a[2 + i]) for i in range(2)]
    q3 = keep_b[1] + over_core(send_b[1])
    q2 = keep_b[2] + over_core(send_b[2])
    q1 = keep_b[3] + over_core(send_b[3])
    p0 = [keep_a[4 + i] + over_core(send_a[4 + i]) for i in range(2)]
    q0 = keep_b[4] + over_core(send_b[4])

    x_in[0] = over_x(add_at(p1[0], x_in[0], 1))
    z_in = over_z(add_at(q3, z_in, 1))
    x_in[1] = over_x(add_at(p1[1], x_in[1], 2))
    z_in = over_z(q2 + z_in)
    near = p0[0] + x_in[0][:3] + over_core(x_in[0][3:])
    v = over_z(near[2:])
    z_in = over_z(q1 + z_in)
    v = over_z(jnp.concatenate([near[1:2] + v, near[:1]]))
    far = p0[1] + x_in[1][:5] + over_core(x_in[1][5:])
    v = over_z(jnp.concatenate([far[4:] + v[:1], far[:1] + v[1:]]))
    b = q0 + z_in[:4] + over_core(z_in[4:])
    w = over_x(b[3:])
    v = over_z(jnp.concatenate([far[3:4] + v[:1], far[1:2] + v[1:]]))
    w = over_x(jnp.concatenate([b[2:3] + w, b[:1]]))
    final_a = far[2] + v[0] + over_core(v[1])
    final_b = b[1] + w[0] + over_core(w[1])

    channels = kernels.shape[1]
    final_a = jnp.transpose(final_a.reshape(COLS[0], GY, channels, 128), (2, 0, 1, 3))
    final_b = jnp.transpose(final_b.reshape(COLS[1], GY, channels, 128), (2, 0, 1, 3))
    projected = jnp.concatenate([final_a, final_b], axis=1)

    even = lat % 2 == 0
    outward = [
        (2 * x + c, 2 * (x + 2 * c - 1) + 1 - c)
        for x in range(CHIPS)
        for c in range(2)
        if 0 <= x + 2 * c - 1 < CHIPS
    ]
    low, high = projected[:, :RADIUS], projected[:, GX - RADIUS :]
    outer = lax.ppermute(jnp.where(even, low, high), "lat", outward)
    inner = over_core(jnp.where(even, high, low))
    along_lat = pass_along(
        jnp.concatenate(
            [jnp.where(even, outer, inner), projected, jnp.where(even, inner, outer)], axis=1
        ),
        1,
    )
    along_lon = pass_along(with_halo(along_lat, "lon", 2, RADIUS), 2)
    smoothed = pass_along(with_halo(along_lon, "dep", 3, RADIUS), 3)
    return (projected, smoothed)


def solution(mesh):
    placed = (
        P(("lat", "lon", "dep"), None, None),
        P(),
        P(("lat", "lon", "dep"), None),
        P(("lat", "lon", "dep")),
        P(("lat", "lon", "dep")),
    )
    return jax.shard_map(
        local,
        mesh=mesh,
        in_specs=placed,
        out_specs=(P(None, "lat", "lon", "dep"), P(None, "lat", "lon", "dep")),
        check_vma=False,
    )
```

```python
import functools
import math

import jax
import jax.numpy as jnp
import numpy as np
from jax import lax
from jax.experimental import pallas as pl
from jax.experimental.pallas import tpu as pltpu
from jax.sharding import PartitionSpec as P

GX = 8
GY = 8
RADIUS = 4
CHIPS = 4
LON = 8
CHUNK = 128
COLS = (5, 3)
GROUP = 4

CORE = [(i, i ^ 1) for i in range(2 * CHIPS)]
RING_X = [(2 * x + c, 2 * ((x + 1 - 2 * c) % CHIPS) + c) for x in range(CHIPS) for c in range(2)]
RING_Z = [
    (lat * LON + z, lat * LON + (z + 1 - 2 * (lat % 2)) % LON)
    for lat in range(2 * CHIPS)
    for z in range(LON)
]

A_P2 = [[(3, 1), (4, 1), (5, 1)], [(0, 1), (1, 1), (2, 1), (6, 1), (7, 1)]]
A_MINE = [[(3, 0), (3, 1), (4, 1)], [(2, 0), (1, 0), (0, 1), (1, 1), (2, 1)]]
A_THEIRS = [[(5, 1), (5, 0), (4, 0)], [(6, 1), (7, 1), (0, 0), (7, 0), (6, 0)]]
LAYOUT_A = (
    [(2, q, own) for part in A_P2 for q, own in part]
    + [(1, q, own) for mine, theirs in zip(A_MINE, A_THEIRS) for q, own in mine + theirs]
    + [(0, q, own) for mine in A_MINE for q, own in mine]
)
B_MINE = [(1, 0), (0, 1), (1, 1), (2, 1)]
B_THEIRS = [(3, 1), (0, 0), (3, 0), (2, 0)]
LAYOUT_B = (
    [(p, 4, 1) for p in range(CHIPS)]
    + [(p, q, own) for q in (3, 2, 1) for p, own in B_MINE + B_THEIRS]
    + [(p, 0, own) for p, own in B_MINE]
)
PARTS_A = (3, 5, 6, 10, 3, 5)
PARTS_B = (4, 8, 8, 8, 4)


def block_tables():
    table = np.zeros((2 * CHIPS, LON, 8, 128), np.int32)
    for lat in range(2 * CHIPS):
        for z in range(LON):
            for owner in range(2 * CHIPS * LON):
                core = owner // LON % 2
                dx = (owner // LON // 2 - lat // 2) % CHIPS
                dz = (owner % LON - z) % LON
                by_x = {0: None, 1: 0, 2: core, 3: 1}[dx]
                by_z = {0: None, 4: core}.get(dz, 0 if dz < 4 else 1)
                for half, (first, second, layout) in enumerate(
                    ((by_x, by_z, LAYOUT_A), (by_z, by_x, LAYOUT_B))
                ):
                    handler = first if first is not None else second if second is not None else core
                    sign = 1 - 2 * handler
                    place = layout.index((dx * sign % CHIPS, dz * sign % LON, int(core == handler)))
                    block = (0 if handler == lat % 2 else 32) + place
                    table[lat, z, half, owner] = GY * (
                        64 * COLS[0] * half + block * COLS[half]
                    )
    return table.reshape(2 * CHIPS * LON, 8, 128)


def project_kernel(
    kernels_ref,
    weights_ref,
    owner_ref,
    column_ref,
    basis_ref,
    me_ref,
    tables_ref,
    acc,
    raw,
    plain,
    stage,
    pos_v,
    row_v,
    end_v,
    pos_s,
    row_s,
    end_s,
    table_s,
    raw_sems,
    sems,
):
    rows, lanes = owner_ref.shape
    basis_count = weights_ref.shape[0]
    channels, elems, _ = kernels_ref.shape
    pitch = plain.shape[0] // channels

    table = pltpu.make_async_copy(tables_ref.at[me_ref[0]], table_s, sems.at[3])
    table.start()
    fetches = [
        pltpu.make_async_copy(kernels_ref.at[c], raw.at[c], raw_sems.at[c])
        for c in range(channels)
    ]
    for fetch in fetches:
        fetch.start()

    basis = basis_ref[...]
    hits = [basis == b for b in range(basis_count)]
    upper = (
        lax.broadcasted_iota(jnp.int32, (lanes, lanes), 0)
        <= lax.broadcasted_iota(jnp.int32, (lanes, lanes), 1)
    ).astype(jnp.float32)
    every = basis_count * rows
    to = lax.broadcasted_iota(jnp.int32, (every, every), 0)
    source = lax.broadcasted_iota(jnp.int32, (every, every), 1)
    lower = ((source < to) & (source // rows == to // rows)).astype(jnp.float32)
    inside = jnp.dot(
        jnp.concatenate([hit.astype(jnp.float32) for hit in hits]),
        upper,
        preferred_element_type=jnp.float32,
    )
    in_row = jnp.broadcast_to(inside[:, lanes - 1 :], (every, lanes))
    before = jnp.dot(lower, in_row, preferred_element_type=jnp.float32)
    ranks = (before + inside).astype(jnp.int32) - 1
    totals = (before + in_row).astype(jnp.int32)
    base = jnp.zeros((1, lanes), jnp.int32)
    pos = jnp.zeros((rows, lanes), jnp.int32)
    for b, hit in enumerate(hits):
        end = (b + 1) * rows
        pos = jnp.where(hit, base + ranks[end - rows : end], pos)
        base = base + (totals[end - 1 : end] + CHUNK - 1) // CHUNK * CHUNK
        end_v[pl.ds(b, 1), :] = base // CHUNK
    pos_v[...] = pos * channels

    owner = owner_ref[...]
    column = column_ref[...]
    first = jnp.zeros((rows, lanes), jnp.int32)
    second = jnp.zeros((rows, lanes), jnp.int32)
    table.wait()
    for o in range(2 * CHIPS * LON):
        hit = owner == o
        first = jnp.where(hit, table_s[0, o], first)
        second = jnp.where(hit, table_s[1, o], second)
    width = GY * COLS[0]
    row = jnp.where(column < width, first + column, second + column - width)
    row_v[...] = row * channels

    loads = [
        pltpu.make_async_copy(source, target, sems.at[i])
        for i, (source, target) in enumerate(
            ((pos_v, pos_s), (row_v, row_s), (end_v, end_s))
        )
    ]
    for load in loads:
        load.start()

    def clear(i, _):
        acc[pl.ds(pl.multiple_of(i * 512, 512), 512), :] = jnp.zeros((512, 128), jnp.float32)
        return 0

    lax.fori_loop(0, acc.shape[0] // 512, clear, 0)

    for c, fetch in enumerate(fetches):
        fetch.wait()

        def widen(i, _):
            start = pl.multiple_of(i * 256, 256)
            plain[pl.ds(c * pitch + start, 256), :] = raw[c, pl.ds(start, 256), :].astype(
                jnp.float32
            )
            return 0

        lax.fori_loop(0, elems // 256, widen, 0)
    for load in loads:
        load.wait()

    def order(r, _):
        for j in range(lanes):
            stage[pl.ds(pos_s[r, j], channels), :] = plain[
                pl.ds(r * lanes + j, channels, stride=pitch), :
            ]
        return 0

    lax.fori_loop(0, rows, order, 0)

    def multiply(b):
        weight = weights_ref[b]

        def one(k, _):
            where = pl.ds(pl.multiple_of(k * (CHUNK * channels), CHUNK * channels), CHUNK * channels)
            stage[where, :] = jnp.dot(
                stage[where, :].astype(jnp.bfloat16), weight, preferred_element_type=jnp.float32
            )
            return 0

        lax.fori_loop(0 if b == 0 else end_s[b - 1, 0], end_s[b, 0], one, 0)

    for b in range(basis_count):
        multiply(b)

    def scatter(r, _):
        for j in range(0, lanes, GROUP):
            targets = [row_s[r, j + i] for i in range(GROUP)]
            sums = [acc[pl.ds(target, channels), :] for target in targets]
            terms = [stage[pl.ds(pos_s[r, j + i], channels), :] for i in range(GROUP)]
            for i in range(GROUP):
                sums[i] = sums[i] + terms[i]
                for h in range(i):
                    sums[i] = sums[i] + jnp.where(targets[i] == targets[h], terms[h], 0.0)
            for target, value in zip(targets, sums):
                acc[pl.ds(target, channels), :] = value
        return 0

    lax.fori_loop(0, rows, scatter, 0)


def project(kernels, basis_weights, owner, column, basis, me, tables):
    elems, channels, points = kernels.shape
    rows = elems // 128
    room = elems + 8 * CHUNK
    pitch = elems + 8
    vmem = pl.BlockSpec(memory_space=pltpu.VMEM)
    total = 64 * GX * GY * channels
    acc = pl.pallas_call(
        project_kernel,
        out_shape=pltpu.VMEM((total, 128), jnp.float32),
        in_specs=[pl.BlockSpec(memory_space=pl.ANY)]
        + [vmem] * 4
        + [pl.BlockSpec(memory_space=pltpu.SMEM), pl.BlockSpec(memory_space=pl.ANY)],
        out_specs=vmem,
        scratch_shapes=[
            pltpu.VMEM((channels, elems, 128), jnp.bfloat16),
            pltpu.VMEM((channels * pitch, 128), jnp.float32),
            pltpu.VMEM((channels * room, 128), jnp.float32),
            pltpu.VMEM((rows, 128), jnp.int32),
            pltpu.VMEM((rows, 128), jnp.int32),
            pltpu.VMEM((8, 128), jnp.int32),
            pltpu.SMEM((rows, 128), jnp.int32),
            pltpu.SMEM((rows, 128), jnp.int32),
            pltpu.SMEM((8, 128), jnp.int32),
            pltpu.SMEM((8, 128), jnp.int32),
            pltpu.SemaphoreType.DMA((channels,)),
            pltpu.SemaphoreType.DMA((4,)),
        ],
        compiler_params=pltpu.CompilerParams(vmem_limit_bytes=48 * 1024 * 1024),
        name="project",
    )(
        jnp.transpose(kernels, (1, 0, 2)),
        basis_weights,
        owner.reshape(rows, 128),
        column.reshape(rows, 128),
        basis.reshape(rows, 128),
        me,
        tables,
    )
    return acc


def part_rows(channels):
    found = []
    start = 0
    for counts, cols in ((PARTS_A, COLS[0]), (PARTS_B, COLS[1])):
        for _ in range(2):
            rows = [count * cols * GY * channels for count in counts]
            found.append([(start + sum(rows[:i]), rows[i]) for i in range(len(rows))])
            start += sum(rows)
    return found


def over_core(value):
    return lax.ppermute(value, "lat", CORE)


def over_x(value):
    return lax.ppermute(value, "lat", RING_X)


def over_z(value):
    return lax.ppermute(value, ("lat", "lon"), RING_Z)


def add_at(block, part, start):
    end = start + part.shape[0]
    return jnp.concatenate([block[:start], block[start:end] + part, block[end:]])


def after(value, *others):
    return lax.optimization_barrier((value, others))[0]


def gauss_taps():
    weights = [math.exp(-(offset * offset) / 8.0) for offset in range(-RADIUS, RADIUS + 1)]
    total = 0.0
    for value in weights:
        total = total + value
    return [value / total for value in weights]


def pass_along(padded, axis_pos):
    length = padded.shape[axis_pos] - 2 * RADIUS
    result = None
    for place, factor in enumerate(gauss_taps()):
        term = factor * lax.slice_in_dim(padded, place, place + length, axis=axis_pos)
        result = term if result is None else result + term
    return result


def steps_along(count):
    pairs = []
    for lat in range(2 * CHIPS):
        for i in range(count):
            j = i + 1 - 2 * (lat % 2)
            if 0 <= j < count:
                pairs.append((lat * count + i, lat * count + j))
    return pairs


def halos(low, high, axis, even):
    other = over_core(jnp.where(even, low, high))
    came = lax.ppermute(
        jnp.stack([jnp.where(even, high, low), other]),
        ("lat", axis),
        steps_along(lax.axis_size(axis)),
    )
    other = over_core(came[1])
    return jnp.where(even, came[0], other), jnp.where(even, other, came[0])


def depth_taps(cells):
    taps = np.zeros((cells + 2 * RADIUS, cells), np.float32)
    for cell in range(cells):
        taps[cell : cell + 2 * RADIUS + 1, cell] = gauss_taps()
    return taps


def local(kernels, basis_weights, owner_block, column_offset, basis_index):
    lat = lax.axis_index("lat")
    lon = lax.axis_index("lon")
    channels = kernels.shape[1]
    acc = project(
        kernels, basis_weights, owner_block, column_offset, basis_index,
        (lat * LON + lon).reshape(1), jnp.asarray(block_tables()),
    )
    ra, rb = (cols * GY * channels for cols in COLS)
    keep_a, send_a, keep_b, send_b = part_rows(channels)

    def span(parts):
        return acc[parts[0][0] : parts[-1][0] + parts[-1][1]]

    def merged(keep, send, *steps):
        value = span(send)
        return span(keep) + over_core(after(value, *steps) if steps else value)

    def met(mine, came, rows):
        return mine + came[:rows] + over_core(came[rows:])

    q = merged(keep_b[:1], send_b[:1])
    p2 = [merged(keep_a[i : i + 1], send_a[i : i + 1]) for i in range(2)]
    x = [over_x(part) for part in p2]
    z = over_z(q)
    p1 = merged(keep_a[2:3], send_a[2:3], q, *p2)
    q3 = merged(keep_b[1:2], send_b[1:2], q, *p2)
    rest_a = merged(keep_a[3:], send_a[3:], p1, q3)
    rest_b = merged(keep_b[2:], send_b[2:], p1, q3)

    step = add_at(p1, x[0], ra)
    x[0] = over_x(step)
    step = add_at(q3, z, rb)
    z = over_z(step)
    step = add_at(rest_a[: 10 * ra], x[1], 2 * ra)
    x[1] = over_x(step)
    step = rest_b[: 8 * rb] + z
    z = over_z(step)
    near = met(rest_a[10 * ra : 13 * ra], x[0], 3 * ra)
    v = over_z(near[2 * ra :])
    step = jnp.concatenate([near[ra : 2 * ra] + v, near[:ra]])
    v = over_z(step)
    step = rest_b[8 * rb : 16 * rb] + after(z, step)
    z = over_z(step)
    far = met(rest_a[13 * ra :], after(x[1], v), 5 * ra)
    step = jnp.concatenate([far[4 * ra :], far[:ra]]) + v
    v = over_z(step)
    b = met(rest_b[16 * rb :], z, 4 * rb)
    w = over_x(b[3 * rb :])
    step = jnp.concatenate([far[3 * ra : 4 * ra], far[ra : 2 * ra]]) + v
    v = over_z(step)
    step = jnp.concatenate([b[2 * rb : 3 * rb] + w, b[:rb]])
    w = over_x(step)
    final_a = far[2 * ra : 3 * ra] + v[:ra] + over_core(v[ra:])
    final_b = b[rb : 2 * rb] + w[:rb] + over_core(w[rb:])

    final_a = jnp.transpose(final_a.reshape(COLS[0], GY, channels, 128), (2, 0, 1, 3))
    final_b = jnp.transpose(final_b.reshape(COLS[1], GY, channels, 128), (2, 0, 1, 3))
    projected = jnp.concatenate([final_a, final_b], axis=1)

    even = lat % 2 == 0
    outward = [
        (2 * x + c, 2 * (x + 2 * c - 1) + 1 - c)
        for x in range(CHIPS)
        for c in range(2)
        if 0 <= x + 2 * c - 1 < CHIPS
    ]
    low, high = projected[:, :RADIUS], projected[:, GX - RADIUS :]
    outer = lax.ppermute(jnp.where(even, low, high), "lat", outward)
    inner = over_core(jnp.where(even, high, low))
    along_lat = pass_along(
        jnp.concatenate(
            [jnp.where(even, outer, inner), projected, jnp.where(even, inner, outer)], axis=1
        ),
        1,
    )
    low, high = halos(along_lat[:, :, :RADIUS], along_lat[:, :, GY - RADIUS :], "lon", even)
    along_lon = pass_along(jnp.concatenate([low, along_lat, high], axis=2), 2)
    flat = along_lon.reshape(channels * GX * GY, -1)
    cells = flat.shape[1]
    low, high = halos(
        jnp.transpose(flat[:, :RADIUS]), jnp.transpose(flat[:, cells - RADIUS :]), "dep", even
    )
    taps = depth_taps(cells)
    inside = jnp.dot(flat, taps[RADIUS : RADIUS + cells], precision=lax.Precision.HIGHEST)
    outside = lax.dot_general(
        jnp.concatenate([low, high]),
        np.concatenate([taps[:RADIUS], taps[RADIUS + cells :]]),
        (((0,), (0,)), ((), ())),
        precision=lax.Precision.HIGHEST,
    )
    smoothed = (inside + outside).reshape(along_lon.shape)
    return (projected, smoothed)


def solution(mesh):
    placed = (
        P(("lat", "lon", "dep"), None, None),
        P(),
        P(("lat", "lon", "dep"), None),
        P(("lat", "lon", "dep")),
        P(("lat", "lon", "dep")),
    )
    return jax.shard_map(
        local,
        mesh=mesh,
        in_specs=placed,
        out_specs=(P(None, "lat", "lon", "dep"), P(None, "lat", "lon", "dep")),
        check_vma=False,
    )
```
